256 devices in a mesh: ctx: 16 (over x_hi, z), fsdp: 16 (over x_lo, y, core).
Axes of the slice: x: 4 (x_hi: 2, x_lo: 2; x = x_hi * 2 + x_lo), y: 4, z: 8, core: 2. Of those that a mesh axis runs over, the one named last changes fastest.
Arguments:
- hidden: bfloat16 [65536, 7168], P(('ctx', 'fsdp')), may hold values from -16 to 16
- qkv_panel: bfloat16 [7168, 768], P('fsdp'), may hold values from -0.0625 to 0.0625
- qkv_scale: bfloat16 [56, 6], replicated, may hold values from 0.5 to 2
- gate_blocks: int32 [16, 4], P('ctx'), may hold values from 0 to 15, as said below
- gate_live: int32 [16, 4], P('ctx'), may hold values from 0 to 1
Outputs:
- attended: bfloat16 [65536, 512], P(('ctx', 'fsdp'))
The draws below stay inside these ranges and needn't reach their ends.
Inputs may be any that keep to these rules, and one draw needn't show every extreme that they name: `gate_blocks`: row c lists c in slot 0 with gate_live 1; for c of 1 or more slot 1 is live too; the slots with gate_live 1 in row c name distinct blocks of 0 to c.
All inputs are finite; a program needn't handle non-finite values.
Results may differ from the reference program's by a relative error of at most 0.02195.
The reference program's roundings to bfloat16 on the way (of `weight`, `projected` and `weights`) count: a program that leaves them out, or rounds other values in their place, can miss the bound.
Values may be sent and summed in bfloat16 or wider, within the bound.
No kernel may reach another device: no remote copies, remote signals or barrier semaphores. Data moves between devices by JAX's collectives and lax.ppermute only.
A program may use at most 128 MiB of HBM per device.

```python
import math
import jax
import jax.numpy as jnp
from jax import lax

D = 7168
HD = 128
HEADS = 4
QB = 128
TOPK = 4
BLOCK = 4096
NBLK = 16
SEQ = 65536
COLS = 768


def gate_lists(key):

    def one_row(block_index):
        row_key = jax.random.fold_in(key, block_index)
        order_key, keep_key = jax.random.split(row_key)
        shuffled = jax.random.permutation(order_key, NBLK).astype(jnp.int32)
        later_flag = (shuffled >= block_index).astype(jnp.int32)
        ranked = shuffled[jnp.argsort(later_flag, stable=True)]
        picked = ranked[:TOPK - 1]
        kept_slots = (jax.random.randint(keep_key, (TOPK - 1,), 0, 4) > 0) | (jnp.arange(TOPK - 1, dtype=jnp.int32) == 0)
        usable = (picked < block_index) & kept_slots
        padding = jnp.minimum(block_index + 1 + jnp.arange(TOPK - 1, dtype=jnp.int32), NBLK - 1)
        chosen_ids = jnp.where(usable, picked, padding)
        block_ids = jnp.concatenate([block_index[None], chosen_ids]).astype(jnp.int32)
        live_flags = jnp.concatenate([jnp.ones((1,), jnp.int32), usable.astype(jnp.int32)])
        return (block_ids, live_flags)
    return jax.vmap(one_row)(jnp.arange(NBLK, dtype=jnp.int32))


def draw_gate_blocks(key, part):
    block_ids, live_flags = gate_lists(key)
    return block_ids


def draw_gate_live(key, part):
    block_ids, live_flags = gate_lists(key)
    return live_flags


def draw_hidden(key, part):
    key = jax.random.fold_in(key, 11)
    base_key = jax.random.fold_in(key, 0)
    drawn = jnp.clip(jax.random.normal(base_key, (SEQ, D), jnp.float32), -6.0, 6.0)
    return drawn.astype(jnp.bfloat16)


def level_of(stream_key, shape, pieces, low, high):
    def one(dim, parts):
        draws = jax.random.uniform(jax.random.fold_in(jax.random.fold_in(stream_key, 6), dim), (parts,), jnp.float32, low / len(pieces), high / len(pieces))
        return jnp.repeat(jnp.exp(draws), shape[dim] // parts).reshape((-1,) + (1,) * (len(shape) - dim - 1))

    factor_of = one(*pieces[0])
    for cut in pieces[1:]:
        factor_of = factor_of * one(*cut)
    return factor_of


def centred(stream_key, extent, spread, most, cuts=(), held_as=jnp.bfloat16):
    array = spread * jax.random.normal(stream_key, extent, jnp.float32)
    if cuts:
        array = array * level_of(stream_key, extent, cuts, -0.22, 0.18)
    return jnp.clip(array, -most, most).astype(held_as)


def setup_inputs(seed: int = 0) -> dict:
    key_of = jax.random.split(jax.random.key(seed), 6)
    return {
        "hidden": draw_hidden(jax.random.fold_in(key_of[5], 71), 0),
        "qkv_panel": centred(key_of[1], (D, COLS), D ** -0.5, 0.0625, ((0, 16),)),
        "qkv_scale": jnp.clip(jnp.exp(jax.random.uniform(key_of[2], (D // QB, HEADS + 2), jnp.float32, math.log(0.5), math.log(2.0))), 0.5, 2.0).astype(jnp.bfloat16),
        "gate_blocks": draw_gate_blocks(jax.random.fold_in(key_of[5], 71), 0),
        "gate_live": draw_gate_live(jax.random.fold_in(key_of[5], 71), 0),
    }


def widen_scale(scale_rows):
    return jnp.repeat(scale_rows.astype(jnp.float32), HD, axis=1)


def reference(hidden, qkv_panel, qkv_scale, gate_blocks, gate_live):
    full_scale = jnp.repeat(widen_scale(qkv_scale), QB, axis=0)
    weight = (qkv_panel.astype(jnp.float32) * full_scale).astype(jnp.bfloat16)
    projected = jnp.dot(hidden, weight, preferred_element_type=jnp.float32).astype(jnp.bfloat16)
    width_q = HEADS * HD
    queries = projected[:, :width_q]
    key_blocks = projected[:, width_q:width_q + HD].reshape(NBLK, BLOCK, HD)
    value_blocks = projected[:, width_q + HD:].reshape(NBLK, BLOCK, HD)
    query_pos = jnp.arange(BLOCK * HEADS, dtype=jnp.int32) // HEADS
    key_slot = jnp.arange(TOPK * BLOCK, dtype=jnp.int32) // BLOCK
    key_pos = jnp.arange(TOPK * BLOCK, dtype=jnp.int32) % BLOCK

    def one_block(block_index):
        query_rows = lax.dynamic_slice_in_dim(queries, block_index * BLOCK, BLOCK, 0).reshape(BLOCK * HEADS, HD)
        block_ids = gate_blocks[block_index]
        live_flags = gate_live[block_index]
        keys_here = key_blocks[block_ids].reshape(TOPK * BLOCK, HD)
        values_here = value_blocks[block_ids].reshape(TOPK * BLOCK, HD)
        scores = jnp.dot(query_rows, keys_here.T, preferred_element_type=jnp.float32) * (HD ** -0.5)
        slot_block = block_ids[key_slot]
        slot_live = live_flags[key_slot]
        allowed = (slot_live[None, :] == 1) & ((slot_block[None, :] != block_index) | (key_pos[None, :] <= query_pos[:, None]))
        highest = jnp.max(jnp.where(allowed, scores, -1e30), axis=1, keepdims=True)
        weights = jnp.exp(jnp.where(allowed, scores - highest, -1e30))
        numer = jnp.dot(weights.astype(jnp.bfloat16), values_here, preferred_element_type=jnp.float32)
        attended_rows = numer / jnp.sum(weights, axis=1, keepdims=True)
        return attended_rows.reshape(BLOCK, HEADS * HD).astype(jnp.bfloat16)

    blocks_out = lax.map(one_block, jnp.arange(NBLK, dtype=jnp.int32))
    return blocks_out.reshape(SEQ, HEADS * HD)
```

```python
import jax
import jax.numpy as jnp
import numpy as np
from jax import lax
from jax.experimental import pallas as pl
from jax.experimental.pallas import tpu as pltpu
from jax.sharding import PartitionSpec as P

HD = 128
HEADS = 4
QB = 128
WIDTH_Q = HEADS * HD
TOKENS = 256
NSLOT = 3
LOG2_SCALE = HD ** -0.5 * 1.4426950408889634
LOW = -1e30
VMEM = 24 * 2 ** 20
f32 = jnp.float32
bf16 = jnp.bfloat16
JOINT = ("ctx", "fsdp")


def plane_pairs(dy=0, dx=0, dcore=0):
    pairs = []
    for i in range(16):
        x, y, core = i >> 3, (i >> 1) & 3, i & 1
        j = ((x ^ dx) << 3) | (((y + dy) % 4) << 1) | (core ^ dcore)
        pairs.append((i, j))
    return pairs


def z_pairs(by):
    return [(i, (i & 8) | ((i + by) % 8)) for i in range(16)]


def joint_pairs(to_x, keep):
    pairs = []
    for i in range(256):
        c, p = i >> 4, i & 15
        if not keep(c >> 3):
            continue
        x2 = to_x(2 * (c >> 3) + (p >> 3)) % 4
        c2 = ((x2 >> 1) << 3) | (c & 7)
        p2 = ((x2 & 1) << 3) | (p & 7)
        pairs.append((i, c2 * 16 + p2))
    return pairs


def by_plane(v, dy=0, dx=0, dcore=0):
    return lax.ppermute(v, "fsdp", plane_pairs(dy, dx, dcore))


def by_x(v, step):
    return lax.ppermute(v, JOINT, joint_pairs(lambda x: x + step, lambda hi: True))


def by_z(v, step):
    return lax.ppermute(v, "ctx", z_pairs(step))


def across(v, from_hi):
    return lax.ppermute(v, JOINT, joint_pairs(lambda x: 3 - x, lambda hi: hi == from_hi))


def spot():
    p = lax.axis_index("fsdp")
    return p // 8, (p // 2) % 4, p % 2


def chip_at(x_lo, y, dx, dy):
    return ((x_lo + dx) % 2) * 4 + (y + dy) % 4


VM = pl.BlockSpec(memory_space=pltpu.VMEM)
SM = pl.BlockSpec(memory_space=pltpu.SMEM)
ANY = pl.BlockSpec(memory_space=pl.ANY)


CHIPS = [(0, 0), (0, -1), (0, 1), (0, 2), (1, 0), (1, -1), (1, 1), (1, 2)]


def kv_project(scales, hidden, sib_hidden, panel, layout, after):
    width = 2 * HD

    def body(scale_ref, h_ref, sib_ref, *refs):
        src, (mine_ref, theirs_ref, w_ref) = refs[:len(panel)], refs[-3:]
        x_lo, y, core = spot()
        for n in range(8):
            at = pl.multiple_of(n * 512 + (1 - core) * 448, 64)
            w_ref[pl.ds(at, 64), :] = jnp.zeros((64, width), bf16)
        for ref, pieces in zip(src, layout):
            for row, rows, n, inside in pieces:
                dx, dy = CHIPS[n]
                first = chip_at(x_lo, y, dx, dy) * 896 + core * 448 + inside
                step = 64 if inside % 64 == 0 and rows % 64 == 0 else 32
                for k in range(rows // step):
                    group = (first + k * step) // QB
                    at = pl.multiple_of(n * 512 + core * 64 + inside + k * step, 32)
                    for c in range(width // HD):
                        lanes = slice(c * HD, (c + 1) * HD)
                        part = ref[row + k * step:row + (k + 1) * step, lanes].astype(f32) * scale_ref[group, HEADS + c]
                        w_ref[pl.ds(at, step), lanes] = part.astype(bf16)
        for tokens, out in ((sib_ref, theirs_ref), (h_ref, mine_ref)):
            acc = None
            for n, (dx, dy) in enumerate(CHIPS):
                lanes = pl.ds(pl.multiple_of(chip_at(x_lo, y, dx, dy) * 896 + core * 384, 128), 512)
                d = jnp.dot(tokens[:, lanes], w_ref[n * 512:(n + 1) * 512, :], preferred_element_type=f32)
                acc = d if acc is None else acc + d
            out[...] = acc

    return pl.pallas_call(
        body,
        in_specs=[SM, VM, VM] + [VM] * len(panel) + [ANY] * len(after),
        out_specs=[VM] * 2,
        out_shape=[jax.ShapeDtypeStruct((TOKENS, width), f32)] * 2,
        scratch_shapes=[pltpu.VMEM((8 * 512, width), bf16)],
        cost_estimate=pl.CostEstimate(
            flops=2 * 256 * 7168 * width, bytes_accessed=8 * 2 ** 20, transcendentals=0),
        compiler_params=pltpu.CompilerParams(vmem_limit_bytes=VMEM),
    )(scales, hidden, sib_hidden, *panel, *after)


def q_project(scales, hidden, panel, after):
    depth = 1024
    steps = 7168 // depth

    def body(scale_ref, h_ref, p_ref, *refs):
        out_ref, w_ref, acc_ref = refs[-3:]
        i = pl.program_id(0)

        @pl.when(i == 0)
        def _():
            acc_ref[...] = jnp.zeros_like(acc_ref)

        for r in range(depth // QB):
            for c in range(HEADS):
                s = scale_ref[i * (depth // QB) + r, c]
                rows, lanes = slice(r * QB, (r + 1) * QB), slice(c * HD, (c + 1) * HD)
                w_ref[rows, lanes] = (p_ref[rows, lanes].astype(f32) * s).astype(bf16)
        acc_ref[...] += jnp.dot(h_ref[...], w_ref[...], preferred_element_type=f32)

        @pl.when(i == steps - 1)
        def _():
            out_ref[...] = acc_ref[...].astype(bf16)

    return pl.pallas_call(
        body,
        grid=(steps,),
        in_specs=[
            pl.BlockSpec(memory_space=pltpu.SMEM),
            pl.BlockSpec((TOKENS, depth), lambda i: (0, i)),
            pl.BlockSpec((depth, WIDTH_Q), lambda i: (i, 0)),
        ] + [ANY] * len(after),
        out_specs=pl.BlockSpec((TOKENS, WIDTH_Q), lambda i: (0, 0)),
        out_shape=jax.ShapeDtypeStruct((TOKENS, WIDTH_Q), bf16),
        scratch_shapes=[pltpu.VMEM((depth, WIDTH_Q), bf16), pltpu.VMEM((TOKENS, WIDTH_Q), f32)],
        cost_estimate=pl.CostEstimate(flops=2 * 256 * 7168 * 512, bytes_accessed=11 * 2 ** 20, transcendentals=0),
        compiler_params=pltpu.CompilerParams(vmem_limit_bytes=VMEM),
    )(scales, hidden, panel, *after)


def choose(gate, their_gate, held, after):
    def body(gate_ref, their_ref, *refs):
        kv = refs[:4] + (refs[4:6],) + refs[6:9]
        own_ref, for_ref = refs[-2:]
        c = lax.axis_index("ctx")
        for s in range(NSLOT):
            for ref, out, hi in ((gate_ref, own_ref, c // 8), (their_ref, for_ref, 0)):
                block = ref[0, 1 + s]
                wanted = (ref[1, 1 + s] == 1) & (block // 8 == hi)
                at = jnp.where(wanted, (c + 8 - block % 8) % 8, 0)
                for j in range(8):
                    @pl.when(at == j)
                    def _(s=s, j=j, out=out):
                        if j == 4:
                            out[s, :128] = kv[4][0][...]
                            out[s, 128:] = kv[4][1][...]
                        else:
                            out[s] = kv[j][...]

    shape = jax.ShapeDtypeStruct((NSLOT, TOKENS, 2 * HD), bf16)
    return pl.pallas_call(
        body,
        in_specs=[SM, SM] + [VM] * 9 + [ANY] * len(after),
        out_specs=[VM, VM],
        out_shape=[shape, shape],
        compiler_params=pltpu.CompilerParams(vmem_limit_bytes=VMEM),
    )(gate, their_gate, *held, *after)


def merge(gate, own, got, after):
    def body(gate_ref, own_ref, got_ref, *rest):
        out_ref = rest[-1]
        hi = lax.axis_index("ctx") // 8
        for s in range(NSLOT):
            here = gate_ref[0, 1 + s] // 8 == hi

            @pl.when(here)
            def _(s=s):
                out_ref[s] = own_ref[s]

            @pl.when(jnp.logical_not(here))
            def _(s=s):
                out_ref[s] = got_ref[s]

    return pl.pallas_call(
        body,
        in_specs=[SM, VM, VM] + [ANY] * len(after),
        out_specs=VM,
        out_shape=jax.ShapeDtypeStruct((NSLOT, TOKENS, 2 * HD), bf16),
        compiler_params=pltpu.CompilerParams(vmem_limit_bytes=VMEM),
    )(gate, own, got, *after)


ROWS = TOKENS * HEADS


def attend(gate, queries, pieces, groups, states, halves, after=()):
    first = states is None
    n_state = 3 * len(halves)
    n_in = 0 if first else n_state

    def body(gate_ref, own_q_ref, sib_q_ref, *refs):
        kv = refs[:len(pieces)]
        out = refs[-n_state:]
        if not first:
            before = refs[len(pieces):len(pieces) + n_state]
        x_lo, y, core = spot()
        for at, half in enumerate(halves):
            peak, total, accum = out[3 * at:3 * at + 3]
            if first:
                peak[...] = jnp.full_like(peak, LOW)
                total[...] = jnp.zeros_like(total)
                accum[...] = jnp.zeros_like(accum)
            else:
                for ref, held in zip((peak, total, accum), before[3 * at:3 * at + 3]):
                    ref[...] = held[...]
            q_tile = (own_q_ref if half == 0 else sib_q_ref)[...]
            q = jnp.concatenate([q_tile[:, h * HD:(h + 1) * HD] for h in range(HEADS)], axis=0)
            holder = chip_at(x_lo, y, 0, 0) * 2 + (core if half == 0 else 1 - core)

            def switched(flag):
                if isinstance(flag, int):
                    on = gate_ref[1, 1 + flag] == 1
                else:
                    shard = chip_at(x_lo, y, *flag) * 2 + core
                    on = (shard < holder) | ((shard == holder) & (half == 0))
                return jnp.where(on, 0.0, LOW).astype(f32)

            for members in groups:
                ts = []
                for flag, piece, index in members:
                    t = lax.dot_general(q, kv[piece][index, :, :HD], (((1,), (1,)), ((), ())),
                                        preferred_element_type=f32) * LOG2_SCALE
                    if flag == (0, 0) and half == 0:
                        row = lax.broadcasted_iota(jnp.int32, t.shape, 0) % TOKENS
                        t = jnp.where(lax.broadcasted_iota(jnp.int32, t.shape, 1) <= row, t, LOW)
                    else:
                        t = t + switched(flag)
                    ts.append(t)
                top = ts[0]
                for t in ts[1:]:
                    top = jnp.maximum(top, t)
                top = jnp.max(jnp.maximum(top[:, :HD], top[:, HD:]), axis=1, keepdims=True)
                old = peak[...]
                new = jnp.maximum(old, jnp.broadcast_to(top, old.shape))
                fade = jnp.exp2(old - new)
                both = jnp.concatenate([new, new], axis=1)
                sums = added = None
                for t, (_, piece, index) in zip(ts, members):
                    w = jnp.exp2(t - both)
                    part = w[:, :HD] + w[:, HD:]
                    d = jnp.dot(w.astype(bf16), kv[piece][index, :, HD:], preferred_element_type=f32)
                    sums = part if sums is None else sums + part
                    added = d if added is None else added + d
                peak[...] = new
                total[...] = total[...] * fade + sums
                accum[...] = accum[...] * fade + added

    n_keys = sum(len(m) for m in groups) * TOKENS
    rows = ROWS * len(halves)
    flat = [] if first else [a for state in states for a in state]
    got = pl.pallas_call(
        body,
        in_specs=[SM, VM, VM] + [VM] * (len(pieces) + n_in) + [ANY] * len(after),
        out_specs=[VM] * n_state,
        out_shape=[jax.ShapeDtypeStruct((ROWS, HD), f32)] * n_state,
        input_output_aliases={} if first else {3 + len(pieces) + n: n for n in range(n_state)},
        cost_estimate=pl.CostEstimate(
            flops=4 * rows * n_keys * HD, bytes_accessed=6 * 2 ** 20, transcendentals=rows * n_keys),
        compiler_params=pltpu.CompilerParams(vmem_limit_bytes=VMEM),
    )(gate, *queries, *pieces, *flat, *after)
    return [got[3 * n:3 * n + 3] for n in range(len(halves))]


def finish(state, got):
    def body(p1, l1, a1, p2, l2, a2, out_ref):
        new = jnp.maximum(p1[...], p2[...])
        f1, f2 = jnp.exp2(p1[...] - new), jnp.exp2(p2[...] - new)
        total = jnp.sum(l1[...] * f1 + l2[...] * f2, axis=1, keepdims=True)
        out = (a1[...] * f1 + a2[...] * f2) / total
        for h in range(HEADS):
            out_ref[:, h * HD:(h + 1) * HD] = out[h * TOKENS:(h + 1) * TOKENS].astype(bf16)

    return pl.pallas_call(
        body,
        in_specs=[VM] * 6,
        out_specs=VM,
        out_shape=jax.ShapeDtypeStruct((TOKENS, WIDTH_Q), bf16),
        compiler_params=pltpu.CompilerParams(vmem_limit_bytes=VMEM),
    )(*state, *got)


def packed(parts, outs, dtype=bf16, after=()):
    shapes = []
    for pieces in outs:
        rows = sum(piece[2] for piece in pieces)
        shapes.append((rows,) + tuple(parts[pieces[0][0]].shape[1:]))

    def body(*refs):
        for out, pieces in zip(refs[len(parts) + len(after):], outs):
            at = 0
            for part, first, rows in pieces:
                out[at:at + rows] = refs[part][first:first + rows]
                at += rows

    return pl.pallas_call(
        body,
        in_specs=[VM] * len(parts) + [ANY] * len(after),
        out_specs=[VM] * len(outs),
        out_shape=[jax.ShapeDtypeStruct(shape, dtype) for shape in shapes],
        compiler_params=pltpu.CompilerParams(vmem_limit_bytes=VMEM),
    )(*parts, *after)


def split_panel(panel):
    def body(panel_ref, own_ref, top_ref, low_ref, queries_ref):
        own_ref[...] = panel_ref[:, WIDTH_Q:]
        top_ref[...] = panel_ref[:224, WIDTH_Q:]
        low_ref[...] = panel_ref[224:, WIDTH_Q:]
        queries_ref[...] = panel_ref[:, :WIDTH_Q]

    shapes = [(448, 2 * HD), (224, 2 * HD), (224, 2 * HD), (448, WIDTH_Q)]
    return pl.pallas_call(
        body,
        in_specs=[VM],
        out_specs=[VM] * 4,
        out_shape=[jax.ShapeDtypeStruct(shape, bf16) for shape in shapes],
        compiler_params=pltpu.CompilerParams(vmem_limit_bytes=VMEM),
    )(panel)


def released(held, after):
    def body(held_ref, after_ref, out_ref):
        pass

    return pl.pallas_call(
        body,
        in_specs=[ANY, ANY],
        out_specs=ANY,
        out_shape=jax.ShapeDtypeStruct(held.shape, held.dtype),
        input_output_aliases={0: 0},
        compiler_params=pltpu.CompilerParams(vmem_limit_bytes=VMEM),
    )(held, after)


PANEL_LAYOUT = [
    [(0, 448, 0, 0)], [(0, 448, 1, 0)], [(0, 448, 2, 0)], [(0, 448, 3, 0)],
    [(0, 224, 4, 0)], [(0, 224, 4, 224)],
    [(0, 224, 5, 0), (224, 224, 6, 0), (448, 224, 7, 0)],
    [(0, 224, 5, 224), (224, 224, 6, 224), (448, 224, 7, 224)],
]


def local(hidden, qkv_panel, qkv_scale, gate_blocks, gate_live):
    scales = qkv_scale.astype(f32)
    gate = jnp.concatenate([gate_blocks, gate_live], axis=0)

    own, top, low, q_columns = split_panel(qkv_panel)
    sib_hidden = by_plane(hidden, dcore=1)
    their_gate = across(gate, 1)
    below, above = by_plane(own, dy=1), by_plane(own, dy=-1)
    x_top, x_low = by_x(top, 1), by_x(low, -1)
    far = by_plane(own, dy=2)
    tops, lows = packed([below, above, far], [[(n, 0, 224) for n in range(3)], [(n, 224, 224) for n in range(3)]],
                        after=[x_top, x_low])
    g_top, g_low = by_x(tops, 1), by_x(lows, -1)
    q_panel = lax.all_gather(released(q_columns, tops), "fsdp", axis=0, tiled=True)
    mine, theirs = kv_project(scales, hidden, sib_hidden, [own, below, above, far, x_top, x_low, g_top, g_low],
                              PANEL_LAYOUT, [their_gate])
    kv = (mine + by_plane(theirs, dcore=1)).astype(bf16)

    z1, z7 = by_z(kv, 1), by_z(kv, -1)
    z2, z6 = by_z(kv, 2), by_z(kv, -2)
    z3, z5 = by_z(z2, 1), by_z(z6, -1)
    z4_top, z4_low = by_z(z2[:128], 2), by_z(z6[128:], -2)

    own_kv, for_partner = choose(gate, their_gate, [kv, z1, z2, z3, z4_top, z4_low, z5, z6, z7], [])

    kv1 = released(kv, for_partner)[None]
    below, above, beside, far = by_plane(kv1, dy=1), by_plane(kv1, dy=-1), by_plane(kv1, dx=1), by_plane(kv1, dy=2)
    packed_pair, = packed([below, above], [[(0, 0, 1), (1, 0, 1)]])
    pair, corner = by_plane(packed_pair, dx=1), by_plane(beside, dy=2)
    near = [kv1, below, above, beside, far, pair, corner]

    q = q_project(scales, hidden, q_panel, [packed_pair, beside, far])
    queries = (q, by_plane(q, dcore=1))
    chosen = merge(gate, own_kv, across(for_partner, 0), [q, pair, corner])
    below, above, beside = by_plane(chosen, dy=1), by_plane(chosen, dy=-1), by_plane(chosen, dx=1)
    states = attend(gate, queries, near[:4], [[((0, 0), 0, 0), ((0, -1), 1, 0), ((0, 1), 2, 0), ((1, 0), 3, 0)]],
                    None, (0, 1), after=[chosen])

    pair, beside2, chosen2 = packed(
        [below, above, beside, chosen],
        [[(0, 0, NSLOT), (1, 0, NSLOT)], [(2, 0, NSLOT)], [(3, 0, NSLOT)]], after=states[0][:1])
    pair, corner, far = by_plane(pair, dx=1), by_plane(beside2, dy=2), by_plane(chosen2, dy=2)
    states = attend(gate, queries, [chosen, below, above, beside] + near[4:],
                    [[(s, n, s) for n in range(4)] for s in range(NSLOT)]
                    + [[((0, 2), 4, 0), ((1, -1), 5, 0), ((1, 1), 5, 1), ((1, 2), 6, 0)]], states, (0, 1))
    rest = [far, pair, corner]
    groups = [[(s, 0, s), (s, 1, s), (s, 1, NSLOT + s), (s, 2, s)] for s in range(NSLOT)]
    sent, = attend(gate, queries, rest, groups, states[1:], (1,))
    got = [by_plane(a, dcore=1) for a in sent]
    kept, = attend(gate, queries, rest, groups, states[:1], (0,), after=sent[:1])
    return finish(kept, got)


def solution(mesh):
    placed = (P(("ctx", "fsdp"), None), P("fsdp", None), P(), P("ctx", None), P("ctx", None))
    return jax.shard_map(
        local, mesh=mesh, in_specs=placed, out_specs=P(("ctx", "fsdp"), None), check_vma=False
    )
```

```python
import jax
import jax.numpy as jnp
import numpy as np
from jax import lax
from jax.experimental import pallas as pl
from jax.experimental.pallas import tpu as pltpu
from jax.sharding import PartitionSpec as P

HD = 128
HEADS = 4
QB = 128
WIDTH_Q = HEADS * HD
TOKENS = 256
NSLOT = 3
LOG2_SCALE = HD ** -0.5 * 1.4426950408889634
LOW = -1e30
VMEM = 24 * 2 ** 20
f32 = jnp.float32
bf16 = jnp.bfloat16
JOINT = ("ctx", "fsdp")


def plane_pairs(dy=0, dx=0, dcore=0):
    pairs = []
    for i in range(16):
        x, y, core = i >> 3, (i >> 1) & 3, i & 1
        j = ((x ^ dx) << 3) | (((y + dy) % 4) << 1) | (core ^ dcore)
        pairs.append((i, j))
    return pairs


def z_pairs(by):
    return [(i, (i & 8) | ((i + by) % 8)) for i in range(16)]


def joint_pairs(to_x, keep):
    pairs = []
    for i in range(256):
        c, p = i >> 4, i & 15
        if not keep(c >> 3):
            continue
        x2 = to_x(2 * (c >> 3) + (p >> 3)) % 4
        c2 = ((x2 >> 1) << 3) | (c & 7)
        p2 = ((x2 & 1) << 3) | (p & 7)
        pairs.append((i, c2 * 16 + p2))
    return pairs


def by_plane(v, dy=0, dx=0, dcore=0):
    return lax.ppermute(v, "fsdp", plane_pairs(dy, dx, dcore))


def by_x(v, step):
    return lax.ppermute(v, JOINT, joint_pairs(lambda x: x + step, lambda hi: True))


def by_z(v, step):
    return lax.ppermute(v, "ctx", z_pairs(step))


def across(v, from_hi):
    return lax.ppermute(v, JOINT, joint_pairs(lambda x: 3 - x, lambda hi: hi == from_hi))


def spot():
    p = lax.axis_index("fsdp")
    return p // 8, (p // 2) % 4, p % 2


def chip_at(x_lo, y, dx, dy):
    return ((x_lo + dx) % 2) * 4 + (y + dy) % 4


VM = pl.BlockSpec(memory_space=pltpu.VMEM)
SM = pl.BlockSpec(memory_space=pltpu.SMEM)
ANY = pl.BlockSpec(memory_space=pl.ANY)


CHIPS = [(0, 0), (0, -1), (0, 1), (0, 2), (1, 0), (1, -1), (1, 1), (1, 2)]


def kv_project(scales, hidden, sib_hidden, panel, layout, after):
    width = 2 * HD

    def body(scale_ref, h_ref, sib_ref, *refs):
        src, (mine_ref, theirs_ref, w_ref) = refs[:len(panel)], refs[-3:]
        x_lo, y, core = spot()
        for n in range(8):
            at = pl.multiple_of(n * 512 + (1 - core) * 448, 64)
            w_ref[pl.ds(at, 64), :] = jnp.zeros((64, width), bf16)
        for ref, pieces in zip(src, layout):
            for row, rows, n, inside in pieces:
                dx, dy = CHIPS[n]
                first = chip_at(x_lo, y, dx, dy) * 896 + core * 448 + inside
                step = 64 if inside % 64 == 0 and rows % 64 == 0 else 32
                for k in range(rows // step):
                    group = (first + k * step) // QB
                    at = pl.multiple_of(n * 512 + core * 64 + inside + k * step, 32)
                    for c in range(width // HD):
                        lanes = slice(c * HD, (c + 1) * HD)
                        part = ref[row + k * step:row + (k + 1) * step, lanes].astype(f32) * scale_ref[group, HEADS + c]
                        w_ref[pl.ds(at, step), lanes] = part.astype(bf16)
        for tokens, out in ((sib_ref, theirs_ref), (h_ref, mine_ref)):
            acc = None
            for n, (dx, dy) in enumerate(CHIPS):
                lanes = pl.ds(pl.multiple_of(chip_at(x_lo, y, dx, dy) * 896 + core * 384, 128), 512)
                d = jnp.dot(tokens[:, lanes], w_ref[n * 512:(n + 1) * 512, :], preferred_element_type=f32)
                acc = d if acc is None else acc + d
            out[...] = acc

    return pl.pallas_call(
        body,
        in_specs=[SM, VM, VM] + [VM] * len(panel) + [ANY] * len(after),
        out_specs=[VM] * 2,
        out_shape=[jax.ShapeDtypeStruct((TOKENS, width), f32)] * 2,
        scratch_shapes=[pltpu.VMEM((8 * 512, width), bf16)],
        cost_estimate=pl.CostEstimate(
            flops=2 * 256 * 7168 * width, bytes_accessed=8 * 2 ** 20, transcendentals=0),
        compiler_params=pltpu.CompilerParams(vmem_limit_bytes=VMEM),
    )(scales, hidden, sib_hidden, *panel, *after)


def q_project(scales, hidden, panel, after):
    depth = 1024
    steps = 7168 // depth

    def body(scale_ref, h_ref, p_ref, *refs):
        out_ref, w_ref, acc_ref = refs[-3:]
        i = pl.program_id(0)

        @pl.when(i == 0)
        def _():
            acc_ref[...] = jnp.zeros_like(acc_ref)

        for r in range(depth // QB):
            for c in range(HEADS):
                s = scale_ref[i * (depth // QB) + r, c]
                rows, lanes = slice(r * QB, (r + 1) * QB), slice(c * HD, (c + 1) * HD)
                w_ref[rows, lanes] = (p_ref[rows, lanes].astype(f32) * s).astype(bf16)
        acc_ref[...] += jnp.dot(h_ref[...], w_ref[...], preferred_element_type=f32)

        @pl.when(i == steps - 1)
        def _():
            out_ref[...] = acc_ref[...].astype(bf16)

    return pl.pallas_call(
        body,
        grid=(steps,),
        in_specs=[
            pl.BlockSpec(memory_space=pltpu.SMEM),
            pl.BlockSpec((TOKENS, depth), lambda i: (0, i)),
            pl.BlockSpec((depth, WIDTH_Q), lambda i: (i, 0)),
        ] + [ANY] * len(after),
        out_specs=pl.BlockSpec((TOKENS, WIDTH_Q), lambda i: (0, 0)),
        out_shape=jax.ShapeDtypeStruct((TOKENS, WIDTH_Q), bf16),
        scratch_shapes=[pltpu.VMEM((depth, WIDTH_Q), bf16), pltpu.VMEM((TOKENS, WIDTH_Q), f32)],
        cost_estimate=pl.CostEstimate(flops=2 * 256 * 7168 * 512, bytes_accessed=11 * 2 ** 20, transcendentals=0),
        compiler_params=pltpu.CompilerParams(vmem_limit_bytes=VMEM),
    )(scales, hidden, panel, *after)


def choose(gate, their_gate, held, after):
    def body(gate_ref, their_ref, *refs):
        kv = refs[:4] + (refs[4:6],) + refs[6:9]
        own_ref, for_ref = refs[-2:]
        c = lax.axis_index("ctx")
        for s in range(NSLOT):
            for ref, out, hi in ((gate_ref, own_ref, c // 8), (their_ref, for_ref, 0)):
                block = ref[0, 1 + s]
                wanted = (ref[1, 1 + s] == 1) & (block // 8 == hi)
                at = jnp.where(wanted, (c + 8 - block % 8) % 8, 0)
                for j in range(8):
                    @pl.when(at == j)
                    def _(s=s, j=j, out=out):
                        if j == 4:
                            out[s, :128] = kv[4][0][...]
                            out[s, 128:] = kv[4][1][...]
                        else:
                            out[s] = kv[j][...]

    shape = jax.ShapeDtypeStruct((NSLOT, TOKENS, 2 * HD), bf16)
    return pl.pallas_call(
        body,
        in_specs=[SM, SM] + [VM] * 9 + [ANY] * len(after),
        out_specs=[VM, VM],
        out_shape=[shape, shape],
        compiler_params=pltpu.CompilerParams(vmem_limit_bytes=VMEM),
    )(gate, their_gate, *held, *after)


def merge(gate, own, got, after):
    def body(gate_ref, own_ref, got_ref, *rest):
        out_ref = rest[-1]
        hi = lax.axis_index("ctx") // 8
        for s in range(NSLOT):
            here = gate_ref[0, 1 + s] // 8 == hi

            @pl.when(here)
            def _(s=s):
                out_ref[s] = own_ref[s]

            @pl.when(jnp.logical_not(here))
            def _(s=s):
                out_ref[s] = got_ref[s]

    return pl.pallas_call(
        body,
        in_specs=[SM, VM, VM] + [ANY] * len(after),
        out_specs=VM,
        out_shape=jax.ShapeDtypeStruct((NSLOT, TOKENS, 2 * HD), bf16),
        compiler_params=pltpu.CompilerParams(vmem_limit_bytes=VMEM),
    )(gate, own, got, *after)


ROWS = TOKENS * HEADS


def attend(gate, queries, pieces, groups, states, halves, after=()):
    first = states is None
    n_state = 3 * len(halves)
    n_in = 0 if first else n_state

    def body(gate_ref, own_q_ref, sib_q_ref, *refs):
        kv = refs[:len(pieces)]
        out = refs[-n_state:]
        if not first:
            before = refs[len(pieces):len(pieces) + n_state]
        x_lo, y, core = spot()
        for at, half in enumerate(halves):
            peak, total, accum = out[3 * at:3 * at + 3]
            if first:
                peak[...] = jnp.full_like(peak, LOW)
                total[...] = jnp.zeros_like(total)
                accum[...] = jnp.zeros_like(accum)
            else:
                for ref, held in zip((peak, total, accum), before[3 * at:3 * at + 3]):
                    ref[...] = held[...]
            q_tile = (own_q_ref if half == 0 else sib_q_ref)[...]
            q = jnp.concatenate([q_tile[:, h * HD:(h + 1) * HD] for h in range(HEADS)], axis=0)
            holder = chip_at(x_lo, y, 0, 0) * 2 + (core if half == 0 else 1 - core)

            def switched(flag):
                if isinstance(flag, int):
                    on = gate_ref[1, 1 + flag] == 1
                else:
                    shard = chip_at(x_lo, y, *flag) * 2 + core
                    on = (shard < holder) | ((shard == holder) & (half == 0))
                return jnp.where(on, 0.0, LOW).astype(f32)

            for members in groups:
                ts = []
                for flag, piece, index in members:
                    t = lax.dot_general(q, kv[piece][index, :, :HD], (((1,), (1,)), ((), ())),
                                        preferred_element_type=f32) * LOG2_SCALE
                    if flag == (0, 0) and half == 0:
                        row = lax.broadcasted_iota(jnp.int32, t.shape, 0) % TOKENS
                        t = jnp.where(lax.broadcasted_iota(jnp.int32, t.shape, 1) <= row, t, LOW)
                    else:
                        t = t + switched(flag)
                    ts.append(t)
                top = ts[0]
                for t in ts[1:]:
                    top = jnp.maximum(top, t)
                top = jnp.max(jnp.maximum(top[:, :HD], top[:, HD:]), axis=1, keepdims=True)
                old = peak[...]
                new = jnp.maximum(old, jnp.broadcast_to(top, old.shape))
                fade = jnp.exp2(old - new)
                both = jnp.concatenate([new, new], axis=1)
                sums = added = None
                for t, (_, piece, index) in zip(ts, members):
                    w = jnp.exp2(t - both)
                    part = w[:, :HD] + w[:, HD:]
                    d = jnp.dot(w.astype(bf16), kv[piece][index, :, HD:], preferred_element_type=f32)
                    sums = part if sums is None else sums + part
                    added = d if added is None else added + d
                peak[...] = new
                total[...] = total[...] * fade + sums
                accum[...] = accum[...] * fade + added

    n_keys = sum(len(m) for m in groups) * TOKENS
    rows = ROWS * len(halves)
    flat = [] if first else [a for state in states for a in state]
    got = pl.pallas_call(
        body,
        in_specs=[SM, VM, VM] + [VM] * (len(pieces) + n_in) + [ANY] * len(after),
        out_specs=[VM] * n_state,
        out_shape=[jax.ShapeDtypeStruct((ROWS, HD), f32)] * n_state,
        input_output_aliases={} if first else {3 + len(pieces) + n: n for n in range(n_state)},
        cost_estimate=pl.CostEstimate(
            flops=4 * rows * n_keys * HD, bytes_accessed=6 * 2 ** 20, transcendentals=rows * n_keys),
        compiler_params=pltpu.CompilerParams(vmem_limit_bytes=VMEM),
    )(gate, *queries, *pieces, *flat, *after)
    return [got[3 * n:3 * n + 3] for n in range(len(halves))]


def finish(state, got):
    def body(p1, l1, a1, p2, l2, a2, out_ref):
        new = jnp.maximum(p1[...], p2[...])
        f1, f2 = jnp.exp2(p1[...] - new), jnp.exp2(p2[...] - new)
        total = jnp.sum(l1[...] * f1 + l2[...] * f2, axis=1, keepdims=True)
        out = (a1[...] * f1 + a2[...] * f2) / total
        for h in range(HEADS):
            out_ref[:, h * HD:(h + 1) * HD] = out[h * TOKENS:(h + 1) * TOKENS].astype(bf16)

    return pl.pallas_call(
        body,
        in_specs=[VM] * 6,
        out_specs=VM,
        out_shape=jax.ShapeDtypeStruct((TOKENS, WIDTH_Q), bf16),
        compiler_params=pltpu.CompilerParams(vmem_limit_bytes=VMEM),
    )(*state, *got)


def packed(parts, outs, dtype=bf16, after=()):
    shapes = []
    for pieces in outs:
        rows = sum(piece[2] for piece in pieces)
        shapes.append((rows,) + tuple(parts[pieces[0][0]].shape[1:]))

    def body(*refs):
        for out, pieces in zip(refs[len(parts) + len(after):], outs):
            at = 0
            for part, first, rows in pieces:
                out[at:at + rows] = refs[part][first:first + rows]
                at += rows

    return pl.pallas_call(
        body,
        in_specs=[VM] * len(parts) + [ANY] * len(after),
        out_specs=[VM] * len(outs),
        out_shape=[jax.ShapeDtypeStruct(shape, dtype) for shape in shapes],
        compiler_params=pltpu.CompilerParams(vmem_limit_bytes=VMEM),
    )(*parts, *after)


def split_panel(panel):
    def body(panel_ref, own_ref, top_ref, low_ref, queries_ref):
        own_ref[...] = panel_ref[:, WIDTH_Q:]
        top_ref[...] = panel_ref[:224, WIDTH_Q:]
        low_ref[...] = panel_ref[224:, WIDTH_Q:]
        queries_ref[...] = panel_ref[:, :WIDTH_Q]

    shapes = [(448, 2 * HD), (224, 2 * HD), (224, 2 * HD), (448, WIDTH_Q)]
    return pl.pallas_call(
        body,
        in_specs=[VM],
        out_specs=[VM] * 4,
        out_shape=[jax.ShapeDtypeStruct(shape, bf16) for shape in shapes],
        compiler_params=pltpu.CompilerParams(vmem_limit_bytes=VMEM),
    )(panel)


def released(held, after):
    def body(held_ref, after_ref, out_ref):
        pass

    return pl.pallas_call(
        body,
        in_specs=[ANY, ANY],
        out_specs=ANY,
        out_shape=jax.ShapeDtypeStruct(held.shape, held.dtype),
        input_output_aliases={0: 0},
        compiler_params=pltpu.CompilerParams(vmem_limit_bytes=VMEM),
    )(held, after)


PANEL_LAYOUT = [
    [(0, 448, 0, 0)], [(0, 448, 1, 0)], [(0, 448, 2, 0)], [(0, 448, 3, 0)],
    [(0, 224, 4, 0)], [(0, 224, 4, 224)],
    [(0, 224, 5, 0), (224, 224, 6, 0), (448, 224, 7, 0)],
    [(0, 224, 5, 224), (224, 224, 6, 224), (448, 224, 7, 224)],
]


def local(hidden, qkv_panel, qkv_scale, gate_blocks, gate_live):
    scales = qkv_scale.astype(f32)
    gate = jnp.concatenate([gate_blocks, gate_live], axis=0)

    own, top, low, q_columns = split_panel(qkv_panel)
    sib_hidden = by_plane(hidden, dcore=1)
    their_gate = across(gate, 1)
    below, above = by_plane(own, dy=1), by_plane(own, dy=-1)
    x_top, x_low = by_x(top, 1), by_x(low, -1)
    far = by_plane(own, dy=2)
    tops, lows = packed([below, above, far], [[(n, 0, 224) for n in range(3)], [(n, 224, 224) for n in range(3)]],
                        after=[x_top, x_low])
    g_top, g_low = by_x(tops, 1), by_x(lows, -1)
    q_panel = lax.all_gather(released(q_columns, tops), "fsdp", axis=0, tiled=True)
    mine, theirs = kv_project(scales, hidden, sib_hidden, [own, below, above, far, x_top, x_low, g_top, g_low],
                              PANEL_LAYOUT, [their_gate])
    kv = (mine + by_plane(theirs, dcore=1)).astype(bf16)

    z1, z7 = by_z(kv, 1), by_z(kv, -1)
    z2, z6 = by_z(kv, 2), by_z(kv, -2)
    z3, z5 = by_z(z2, 1), by_z(z6, -1)
    z4_top, z4_low = by_z(z2[:128], 2), by_z(z6[128:], -2)

    own_kv, for_partner = choose(gate, their_gate, [kv, z1, z2, z3, z4_top, z4_low, z5, z6, z7], [])

    kv1 = released(kv, for_partner)[None]
    below, above, beside, far = by_plane(kv1, dy=1), by_plane(kv1, dy=-1), by_plane(kv1, dx=1), by_plane(kv1, dy=2)
    packed_pair, = packed([below, above], [[(0, 0, 1), (1, 0, 1)]])
    pair, corner = by_plane(packed_pair, dx=1), by_plane(beside, dy=2)
    near = [kv1, below, above, beside, far, pair, corner]

    chosen = merge(gate, own_kv, across(for_partner, 0), [pair, corner])
    below, above, beside = by_plane(chosen, dy=1), by_plane(chosen, dy=-1), by_plane(chosen, dx=1)
    q = q_project(scales, hidden, q_panel, [chosen])
    queries = (q, by_plane(q, dcore=1))
    packed_pair, beside2, chosen2 = packed(
        [below, above, beside, chosen],
        [[(0, 0, NSLOT), (1, 0, NSLOT)], [(2, 0, NSLOT)], [(3, 0, NSLOT)]], after=queries[1:])
    held = near + [chosen, below, above, beside]
    states = attend(gate, queries, held,
                    [[((0, 0), 0, 0), ((0, -1), 1, 0), ((0, 1), 2, 0), ((1, 0), 3, 0)],
                     [((0, 2), 4, 0), ((1, -1), 5, 0), ((1, 1), 5, 1), ((1, 2), 6, 0)]]
                    + [[(s, 7 + n, s) for n in range(4)] for s in range(NSLOT)],
                    None, (0, 1), after=[packed_pair])
    pair, corner, far = by_plane(packed_pair, dx=1), by_plane(beside2, dy=2), by_plane(chosen2, dy=2)
    rest = [far, pair, corner]
    groups = [[(s, 0, s), (s, 1, s), (s, 1, NSLOT + s), (s, 2, s)] for s in range(NSLOT)]
    sent, = attend(gate, queries, rest, groups, states[1:], (1,))
    got = [by_plane(a, dcore=1) for a in sent]
    kept, = attend(gate, queries, rest, groups, states[:1], (0,), after=sent[:1])
    return finish(kept, got)


def solution(mesh):
    placed = (P(("ctx", "fsdp"), None), P("fsdp", None), P(), P("ctx", None), P("ctx", None))
    return jax.shard_map(
        local, mesh=mesh, in_specs=placed, out_specs=P(("ctx", "fsdp"), None), check_vma=False
    )
```

```python
import jax
import jax.numpy as jnp
import numpy as np
from jax import lax
from jax.experimental import pallas as pl
from jax.experimental.pallas import tpu as pltpu
from jax.sharding import PartitionSpec as P

HD = 128
HEADS = 4
QB = 128
WIDTH_Q = HEADS * HD
TOKENS = 256
NSLOT = 3
LOG2_SCALE = HD ** -0.5 * 1.4426950408889634
LOW = -1e30
VMEM = 24 * 2 ** 20
f32 = jnp.float32
bf16 = jnp.bfloat16
JOINT = ("ctx", "fsdp")


def plane_pairs(dy=0, dx=0, dcore=0):
    pairs = []
    for i in range(16):
        x, y, core = i >> 3, (i >> 1) & 3, i & 1
        j = ((x ^ dx) << 3) | (((y + dy) % 4) << 1) | (core ^ dcore)
        pairs.append((i, j))
    return pairs


def z_pairs(by):
    return [(i, (i & 8) | ((i + by) % 8)) for i in range(16)]


def joint_pairs(to_x, keep):
    pairs = []
    for i in range(256):
        c, p = i >> 4, i & 15
        if not keep(c >> 3):
            continue
        x2 = to_x(2 * (c >> 3) + (p >> 3)) % 4
        c2 = ((x2 >> 1) << 3) | (c & 7)
        p2 = ((x2 & 1) << 3) | (p & 7)
        pairs.append((i, c2 * 16 + p2))
    return pairs


def by_plane(v, dy=0, dx=0, dcore=0):
    return lax.ppermute(v, "fsdp", plane_pairs(dy, dx, dcore))


def by_x(v, step):
    return lax.ppermute(v, JOINT, joint_pairs(lambda x: x + step, lambda hi: True))


def by_z(v, step):
    return lax.ppermute(v, "ctx", z_pairs(step))


def across(v, from_hi):
    return lax.ppermute(v, JOINT, joint_pairs(lambda x: 3 - x, lambda hi: hi == from_hi))


def spot():
    p = lax.axis_index("fsdp")
    return p // 8, (p // 2) % 4, p % 2


def chip_at(x_lo, y, dx, dy):
    return ((x_lo + dx) % 2) * 4 + (y + dy) % 4


VM = pl.BlockSpec(memory_space=pltpu.VMEM)
SM = pl.BlockSpec(memory_space=pltpu.SMEM)
ANY = pl.BlockSpec(memory_space=pl.ANY)


CHIPS = [(0, 0), (0, -1), (0, 1), (0, 2), (1, 0), (1, -1), (1, 1), (1, 2)]


def kv_project(scales, hidden, sib_hidden, panel, layout, after):
    width = 2 * HD

    def body(scale_ref, h_ref, sib_ref, *refs):
        src, (mine_ref, theirs_ref, w_ref) = refs[:len(panel)], refs[-3:]
        x_lo, y, core = spot()
        for n in range(8):
            at = pl.multiple_of(n * 512 + (1 - core) * 448, 64)
            w_ref[pl.ds(at, 64), :] = jnp.zeros((64, width), bf16)
        for ref, pieces in zip(src, layout):
            for row, rows, n, inside in pieces:
                dx, dy = CHIPS[n]
                first = chip_at(x_lo, y, dx, dy) * 896 + core * 448 + inside
                step = 64 if inside % 64 == 0 and rows % 64 == 0 else 32
                for k in range(rows // step):
                    group = (first + k * step) // QB
                    at = pl.multiple_of(n * 512 + core * 64 + inside + k * step, 32)
                    for c in range(width // HD):
                        lanes = slice(c * HD, (c + 1) * HD)
                        part = ref[row + k * step:row + (k + 1) * step, lanes].astype(f32) * scale_ref[group, HEADS + c]
                        w_ref[pl.ds(at, step), lanes] = part.astype(bf16)
        for tokens, out in ((sib_ref, theirs_ref), (h_ref, mine_ref)):
            acc = None
            for n, (dx, dy) in enumerate(CHIPS):
                lanes = pl.ds(pl.multiple_of(chip_at(x_lo, y, dx, dy) * 896 + core * 384, 128), 512)
                d = jnp.dot(tokens[:, lanes], w_ref[n * 512:(n + 1) * 512, :], preferred_element_type=f32)
                acc = d if acc is None else acc + d
            out[...] = acc

    return pl.pallas_call(
        body,
        in_specs=[SM, VM, VM] + [VM] * len(panel) + [ANY] * len(after),
        out_specs=[VM] * 2,
        out_shape=[jax.ShapeDtypeStruct((TOKENS, width), f32)] * 2,
        scratch_shapes=[pltpu.VMEM((8 * 512, width), bf16)],
        cost_estimate=pl.CostEstimate(
            flops=2 * 256 * 7168 * width, bytes_accessed=8 * 2 ** 20, transcendentals=0),
        compiler_params=pltpu.CompilerParams(vmem_limit_bytes=VMEM),
    )(scales, hidden, sib_hidden, *panel, *after)


def q_project(scales, hidden, panel, after):
    depth = 1024
    steps = 7168 // depth

    def body(scale_ref, h_ref, p_ref, *refs):
        out_ref, w_ref, acc_ref = refs[-3:]
        i = pl.program_id(0)

        @pl.when(i == 0)
        def _():
            acc_ref[...] = jnp.zeros_like(acc_ref)

        for r in range(depth // QB):
            for c in range(HEADS):
                s = scale_ref[i * (depth // QB) + r, c]
                rows, lanes = slice(r * QB, (r + 1) * QB), slice(c * HD, (c + 1) * HD)
                w_ref[rows, lanes] = (p_ref[rows, lanes].astype(f32) * s).astype(bf16)
        acc_ref[...] += jnp.dot(h_ref[...], w_ref[...], preferred_element_type=f32)

        @pl.when(i == steps - 1)
        def _():
            out_ref[...] = acc_ref[...].astype(bf16)

    return pl.pallas_call(
        body,
        grid=(steps,),
        in_specs=[
            pl.BlockSpec(memory_space=pltpu.SMEM),
            pl.BlockSpec((TOKENS, depth), lambda i: (0, i)),
            pl.BlockSpec((depth, WIDTH_Q), lambda i: (i, 0)),
        ] + [ANY] * len(after),
        out_specs=pl.BlockSpec((TOKENS, WIDTH_Q), lambda i: (0, 0)),
        out_shape=jax.ShapeDtypeStruct((TOKENS, WIDTH_Q), bf16),
        scratch_shapes=[pltpu.VMEM((depth, WIDTH_Q), bf16), pltpu.VMEM((TOKENS, WIDTH_Q), f32)],
        cost_estimate=pl.CostEstimate(flops=2 * 256 * 7168 * 512, bytes_accessed=11 * 2 ** 20, transcendentals=0),
        compiler_params=pltpu.CompilerParams(vmem_limit_bytes=VMEM),
    )(scales, hidden, panel, *after)


def choose(gate, their_gate, held, after):
    def body(gate_ref, their_ref, *refs):
        kv = refs[:4] + (refs[4:6],) + refs[6:9]
        own_ref, for_ref = refs[-2:]
        c = lax.axis_index("ctx")
        for s in range(NSLOT):
            for ref, out, hi in ((gate_ref, own_ref, c // 8), (their_ref, for_ref, 0)):
                block = ref[0, 1 + s]
                wanted = (ref[1, 1 + s] == 1) & (block // 8 == hi)
                at = jnp.where(wanted, (c + 8 - block % 8) % 8, 0)
                for j in range(8):
                    @pl.when(at == j)
                    def _(s=s, j=j, out=out):
                        if j == 4:
                            out[s, :128] = kv[4][0][...]
                            out[s, 128:] = kv[4][1][...]
                        else:
                            out[s] = kv[j][...]

    shape = jax.ShapeDtypeStruct((NSLOT, TOKENS, 2 * HD), bf16)
    return pl.pallas_call(
        body,
        in_specs=[SM, SM] + [VM] * 9 + [ANY] * len(after),
        out_specs=[VM, VM],
        out_shape=[shape, shape],
        compiler_params=pltpu.CompilerParams(vmem_limit_bytes=VMEM),
    )(gate, their_gate, *held, *after)


def merge(gate, own, got, after):
    def body(gate_ref, own_ref, got_ref, *rest):
        out_ref = rest[-1]
        hi = lax.axis_index("ctx") // 8
        for s in range(NSLOT):
            here = gate_ref[0, 1 + s] // 8 == hi

            @pl.when(here)
            def _(s=s):
                out_ref[s] = own_ref[s]

            @pl.when(jnp.logical_not(here))
            def _(s=s):
                out_ref[s] = got_ref[s]

    return pl.pallas_call(
        body,
        in_specs=[SM, VM, VM] + [ANY] * len(after),
        out_specs=VM,
        out_shape=jax.ShapeDtypeStruct((NSLOT, TOKENS, 2 * HD), bf16),
        compiler_params=pltpu.CompilerParams(vmem_limit_bytes=VMEM),
    )(gate, own, got, *after)


ROWS = TOKENS * HEADS


def attend(gate, queries, pieces, groups, states, halves, after=()):
    first = states is None
    n_state = 3 * len(halves)
    n_in = 0 if first else n_state

    def body(gate_ref, own_q_ref, sib_q_ref, *refs):
        kv = refs[:len(pieces)]
        out = refs[-n_state:]
        if not first:
            before = refs[len(pieces):len(pieces) + n_state]
        x_lo, y, core = spot()
        for at, half in enumerate(halves):
            peak, total, accum = out[3 * at:3 * at + 3]
            if first:
                peak[...] = jnp.full_like(peak, LOW)
                total[...] = jnp.zeros_like(total)
                accum[...] = jnp.zeros_like(accum)
            else:
                for ref, held in zip((peak, total, accum), before[3 * at:3 * at + 3]):
                    ref[...] = held[...]
            q_tile = (own_q_ref if half == 0 else sib_q_ref)[...]
            q = jnp.concatenate([q_tile[:, h * HD:(h + 1) * HD] for h in range(HEADS)], axis=0)
            holder = chip_at(x_lo, y, 0, 0) * 2 + (core if half == 0 else 1 - core)

            def switched(flag):
                if isinstance(flag, int):
                    on = gate_ref[1, 1 + flag] == 1
                else:
                    shard = chip_at(x_lo, y, *flag) * 2 + core
                    on = (shard < holder) | ((shard == holder) & (half == 0))
                return jnp.where(on, 0.0, LOW).astype(f32)

            for members in groups:
                ts = []
                for flag, piece, index in members:
                    t = lax.dot_general(q, kv[piece][index, :, :HD], (((1,), (1,)), ((), ())),
                                        preferred_element_type=f32) * LOG2_SCALE
                    if flag == (0, 0) and half == 0:
                        row = lax.broadcasted_iota(jnp.int32, t.shape, 0) % TOKENS
                        t = jnp.where(lax.broadcasted_iota(jnp.int32, t.shape, 1) <= row, t, LOW)
                    else:
                        t = t + switched(flag)
                    ts.append(t)
                top = ts[0]
                for t in ts[1:]:
                    top = jnp.maximum(top, t)
                top = jnp.max(jnp.maximum(top[:, :HD], top[:, HD:]), axis=1, keepdims=True)
                old = peak[...]
                new = jnp.maximum(old, jnp.broadcast_to(top, old.shape))
                fade = jnp.exp2(old - new)
                both = jnp.concatenate([new, new], axis=1)
                sums = added = None
                for t, (_, piece, index) in zip(ts, members):
                    w = jnp.exp2(t - both)
                    part = w[:, :HD] + w[:, HD:]
                    d = jnp.dot(w.astype(bf16), kv[piece][index, :, HD:], preferred_element_type=f32)
                    sums = part if sums is None else sums + part
                    added = d if added is None else added + d
                peak[...] = new
                total[...] = total[...] * fade + sums
                accum[...] = accum[...] * fade + added

    n_keys = sum(len(m) for m in groups) * TOKENS
    rows = ROWS * len(halves)
    flat = [] if first else [a for state in states for a in state]
    got = pl.pallas_call(
        body,
        in_specs=[SM, VM, VM] + [VM] * (len(pieces) + n_in) + [ANY] * len(after),
        out_specs=[VM] * n_state,
        out_shape=[jax.ShapeDtypeStruct((ROWS, HD), f32)] * n_state,
        input_output_aliases={} if first else {3 + len(pieces) + n: n for n in range(n_state)},
        cost_estimate=pl.CostEstimate(
            flops=4 * rows * n_keys * HD, bytes_accessed=6 * 2 ** 20, transcendentals=rows * n_keys),
        compiler_params=pltpu.CompilerParams(vmem_limit_bytes=VMEM),
    )(gate, *queries, *pieces, *flat, *after)
    return [got[3 * n:3 * n + 3] for n in range(len(halves))]


def finish(state, got):
    def body(p1, l1, a1, p2, l2, a2, out_ref):
        new = jnp.maximum(p1[...], p2[...])
        f1, f2 = jnp.exp2(p1[...] - new), jnp.exp2(p2[...] - new)
        total = jnp.sum(l1[...] * f1 + l2[...] * f2, axis=1, keepdims=True)
        out = (a1[...] * f1 + a2[...] * f2) / total
        for h in range(HEADS):
            out_ref[:, h * HD:(h + 1) * HD] = out[h * TOKENS:(h + 1) * TOKENS].astype(bf16)

    return pl.pallas_call(
        body,
        in_specs=[VM] * 6,
        out_specs=VM,
        out_shape=jax.ShapeDtypeStruct((TOKENS, WIDTH_Q), bf16),
        compiler_params=pltpu.CompilerParams(vmem_limit_bytes=VMEM),
    )(*state, *got)


def packed(parts, outs, dtype=bf16, after=()):
    shapes = []
    for pieces in outs:
        rows = sum(piece[2] for piece in pieces)
        shapes.append((rows,) + tuple(parts[pieces[0][0]].shape[1:]))

    def body(*refs):
        for out, pieces in zip(refs[len(parts) + len(after):], outs):
            at = 0
            for part, first, rows in pieces:
                out[at:at + rows] = refs[part][first:first + rows]
                at += rows

    return pl.pallas_call(
        body,
        in_specs=[VM] * len(parts) + [ANY] * len(after),
        out_specs=[VM] * len(outs),
        out_shape=[jax.ShapeDtypeStruct(shape, dtype) for shape in shapes],
        compiler_params=pltpu.CompilerParams(vmem_limit_bytes=VMEM),
    )(*parts, *after)


def split_panel(panel):
    def body(panel_ref, own_ref, top_ref, low_ref, queries_ref):
        own_ref[...] = panel_ref[:, WIDTH_Q:]
        top_ref[...] = panel_ref[:224, WIDTH_Q:]
        low_ref[...] = panel_ref[224:, WIDTH_Q:]
        queries_ref[...] = panel_ref[:, :WIDTH_Q]

    shapes = [(448, 2 * HD), (224, 2 * HD), (224, 2 * HD), (448, WIDTH_Q)]
    return pl.pallas_call(
        body,
        in_specs=[VM],
        out_specs=[VM] * 4,
        out_shape=[jax.ShapeDtypeStruct(shape, bf16) for shape in shapes],
        compiler_params=pltpu.CompilerParams(vmem_limit_bytes=VMEM),
    )(panel)


def released(held, after):
    def body(held_ref, after_ref, out_ref):
        pass

    return pl.pallas_call(
        body,
        in_specs=[ANY, ANY],
        out_specs=ANY,
        out_shape=jax.ShapeDtypeStruct(held.shape, held.dtype),
        input_output_aliases={0: 0},
        compiler_params=pltpu.CompilerParams(vmem_limit_bytes=VMEM),
    )(held, after)


PANEL_LAYOUT = [
    [(0, 448, 0, 0)], [(0, 448, 1, 0)], [(0, 448, 2, 0)], [(0, 448, 3, 0)],
    [(0, 224, 4, 0)], [(0, 224, 4, 224)],
    [(0, 224, 5, 0), (224, 224, 6, 0), (448, 224, 7, 0)],
    [(0, 224, 5, 224), (224, 224, 6, 224), (448, 224, 7, 224)],
]


def local(hidden, qkv_panel, qkv_scale, gate_blocks, gate_live):
    scales = qkv_scale.astype(f32)
    gate = jnp.concatenate([gate_blocks, gate_live], axis=0)

    own, top, low, q_columns = split_panel(qkv_panel)
    sib_hidden = by_plane(hidden, dcore=1)
    their_gate = across(gate, 1)
    below, above = by_plane(own, dy=1), by_plane(own, dy=-1)
    x_top, x_low = by_x(top, 1), by_x(low, -1)
    far = by_plane(own, dy=2)
    tops, lows = packed([below, above, far], [[(n, 0, 224) for n in range(3)], [(n, 224, 224) for n in range(3)]],
                        after=[x_top, x_low])
    g_top, g_low = by_x(tops, 1), by_x(lows, -1)
    q_panel = lax.all_gather(released(q_columns, tops), "fsdp", axis=0, tiled=True)
    mine, theirs = kv_project(scales, hidden, sib_hidden, [own, below, above, far, x_top, x_low, g_top, g_low],
                              PANEL_LAYOUT, [their_gate])
    kv = (mine + by_plane(theirs, dcore=1)).astype(bf16)

    z1, z7 = by_z(kv, 1), by_z(kv, -1)
    z2, z6 = by_z(kv, 2), by_z(kv, -2)
    z3, z5 = by_z(z2, 1), by_z(z6, -1)
    z4_top, z4_low = by_z(z2[:128], 2), by_z(z6[128:], -2)

    own_kv, for_partner = choose(gate, their_gate, [kv, z1, z2, z3, z4_top, z4_low, z5, z6, z7], [])

    kv1 = released(kv, for_partner)[None]
    below, above, beside, far = by_plane(kv1, dy=1), by_plane(kv1, dy=-1), by_plane(kv1, dx=1), by_plane(kv1, dy=2)
    packed_pair, = packed([below, above], [[(0, 0, 1), (1, 0, 1)]])
    pair, corner = by_plane(packed_pair, dx=1), by_plane(beside, dy=2)
    near = [kv1, below, above, beside, far, pair, corner]

    chosen = merge(gate, own_kv, across(for_partner, 0), [packed_pair, beside, far])
    below, above, beside = by_plane(chosen, dy=1), by_plane(chosen, dy=-1), by_plane(chosen, dx=1)
    q = q_project(scales, hidden, q_panel, [chosen])
    queries = (q, by_plane(q, dcore=1))
    packed_pair, beside2, chosen2 = packed(
        [below, above, beside, chosen],
        [[(0, 0, NSLOT), (1, 0, NSLOT)], [(2, 0, NSLOT)], [(3, 0, NSLOT)]], after=[queries[1], pair, corner])
    held = near + [chosen, below, above, beside]
    states = attend(gate, queries, held,
                    [[((0, 0), 0, 0), ((0, -1), 1, 0), ((0, 1), 2, 0), ((1, 0), 3, 0)],
                     [((0, 2), 4, 0), ((1, -1), 5, 0), ((1, 1), 5, 1), ((1, 2), 6, 0)]]
                    + [[(s, 7 + n, s) for n in range(4)] for s in range(NSLOT)],
                    None, (0, 1), after=[packed_pair])
    pair, corner, far = by_plane(packed_pair, dx=1), by_plane(beside2, dy=2), by_plane(chosen2, dy=2)
    rest = [far, pair, corner]
    groups = [[(s, 0, s), (s, 1, s), (s, 1, NSLOT + s), (s, 2, s)] for s in range(NSLOT)]
    sent, = attend(gate, queries, rest, groups, states[1:], (1,))
    got = [by_plane(a, dcore=1) for a in sent]
    kept, = attend(gate, queries, rest, groups, states[:1], (0,), after=sent[:1])
    return finish(kept, got)


def solution(mesh):
    placed = (P(("ctx", "fsdp"), None), P("fsdp", None), P(), P("ctx", None), P("ctx", None))
    return jax.shard_map(
        local, mesh=mesh, in_specs=placed, out_specs=P(("ctx", "fsdp"), None), check_vma=False
    )
```

```python
import jax
import jax.numpy as jnp
import numpy as np
from jax import lax
from jax.experimental import pallas as pl
from jax.experimental.pallas import tpu as pltpu
from jax.sharding import PartitionSpec as P

HD = 128
HEADS = 4
QB = 128
WIDTH_Q = HEADS * HD
TOKENS = 256
NSLOT = 3
LOG2_SCALE = HD ** -0.5 * 1.4426950408889634
LOW = -1e30
VMEM = 24 * 2 ** 20
f32 = jnp.float32
bf16 = jnp.bfloat16
JOINT = ("ctx", "fsdp")


def plane_pairs(dy=0, dx=0, dcore=0):
    pairs = []
    for i in range(16):
        x, y, core = i >> 3, (i >> 1) & 3, i & 1
        j = ((x ^ dx) << 3) | (((y + dy) % 4) << 1) | (core ^ dcore)
        pairs.append((i, j))
    return pairs


def z_pairs(by):
    return [(i, (i & 8) | ((i + by) % 8)) for i in range(16)]


def joint_pairs(to_x, keep):
    pairs = []
    for i in range(256):
        c, p = i >> 4, i & 15
        if not keep(c >> 3):
            continue
        x2 = to_x(2 * (c >> 3) + (p >> 3)) % 4
        c2 = ((x2 >> 1) << 3) | (c & 7)
        p2 = ((x2 & 1) << 3) | (p & 7)
        pairs.append((i, c2 * 16 + p2))
    return pairs


def by_plane(v, dy=0, dx=0, dcore=0):
    return lax.ppermute(v, "fsdp", plane_pairs(dy, dx, dcore))


def by_x(v, step):
    return lax.ppermute(v, JOINT, joint_pairs(lambda x: x + step, lambda hi: True))


def by_z(v, step):
    return lax.ppermute(v, "ctx", z_pairs(step))


def across(v, from_hi):
    return lax.ppermute(v, JOINT, joint_pairs(lambda x: 3 - x, lambda hi: hi == from_hi))


def spot():
    p = lax.axis_index("fsdp")
    return p // 8, (p // 2) % 4, p % 2


def chip_at(x_lo, y, dx, dy):
    return ((x_lo + dx) % 2) * 4 + (y + dy) % 4


VM = pl.BlockSpec(memory_space=pltpu.VMEM)
SM = pl.BlockSpec(memory_space=pltpu.SMEM)
ANY = pl.BlockSpec(memory_space=pl.ANY)


CHIPS = [(0, 0), (0, -1), (0, 1), (0, 2), (1, 0), (1, -1), (1, 1), (1, 2)]


def kv_project(scales, hidden, sib_hidden, panel, layout, chips, before, after):
    width = 2 * HD

    def body(scale_ref, h_ref, sib_ref, *refs):
        src, (mine_ref, theirs_ref, w_ref) = refs[:len(panel)], refs[-3:]
        sums = refs[len(panel):len(panel) + len(before)]
        x_lo, y, core = spot()
        for n in range(len(chips)):
            at = pl.multiple_of(n * 512 + (1 - core) * 448, 64)
            w_ref[pl.ds(at, 64), :] = jnp.zeros((64, width), bf16)
        for ref, pieces in zip(src, layout):
            for row, rows, n, inside in pieces:
                dx, dy = CHIPS[n]
                first = chip_at(x_lo, y, dx, dy) * 896 + core * 448 + inside
                step = 64 if inside % 64 == 0 and rows % 64 == 0 else 32
                for k in range(rows // step):
                    group = (first + k * step) // QB
                    at = pl.multiple_of(chips.index(n) * 512 + core * 64 + inside + k * step, 32)
                    for c in range(width // HD):
                        lanes = slice(c * HD, (c + 1) * HD)
                        part = ref[row + k * step:row + (k + 1) * step, lanes].astype(f32) * scale_ref[group, HEADS + c]
                        w_ref[pl.ds(at, step), lanes] = part.astype(bf16)
        for side, tokens, out in ((1, sib_ref, theirs_ref), (0, h_ref, mine_ref)):
            acc = sums[side][...] if before else None
            for at, n in enumerate(chips):
                dx, dy = CHIPS[n]
                lanes = pl.ds(pl.multiple_of(chip_at(x_lo, y, dx, dy) * 896 + core * 384, 128), 512)
                d = jnp.dot(tokens[:, lanes], w_ref[at * 512:(at + 1) * 512, :], preferred_element_type=f32)
                acc = d if acc is None else acc + d
            out[...] = acc

    return pl.pallas_call(
        body,
        in_specs=[SM, VM, VM] + [VM] * (len(panel) + len(before)) + [ANY] * len(after),
        out_specs=[VM] * 2,
        out_shape=[jax.ShapeDtypeStruct((TOKENS, width), f32)] * 2,
        scratch_shapes=[pltpu.VMEM((len(chips) * 512, width), bf16)],
        cost_estimate=pl.CostEstimate(
            flops=2 * 512 * 512 * len(chips) * width, bytes_accessed=8 * 2 ** 20, transcendentals=0),
        compiler_params=pltpu.CompilerParams(vmem_limit_bytes=VMEM),
    )(scales, hidden, sib_hidden, *panel, *before, *after)


def q_project(scales, hidden, panel, after):
    depth = 1024
    steps = 7168 // depth

    def body(scale_ref, h_ref, p_ref, *refs):
        out_ref, w_ref, acc_ref = refs[-3:]
        i = pl.program_id(0)

        @pl.when(i == 0)
        def _():
            acc_ref[...] = jnp.zeros_like(acc_ref)

        for r in range(depth // QB):
            for c in range(HEADS):
                s = scale_ref[i * (depth // QB) + r, c]
                rows, lanes = slice(r * QB, (r + 1) * QB), slice(c * HD, (c + 1) * HD)
                w_ref[rows, lanes] = (p_ref[rows, lanes].astype(f32) * s).astype(bf16)
        acc_ref[...] += jnp.dot(h_ref[...], w_ref[...], preferred_element_type=f32)

        @pl.when(i == steps - 1)
        def _():
            out_ref[...] = acc_ref[...].astype(bf16)

    return pl.pallas_call(
        body,
        grid=(steps,),
        in_specs=[
            pl.BlockSpec(memory_space=pltpu.SMEM),
            pl.BlockSpec((TOKENS, depth), lambda i: (0, i)),
            pl.BlockSpec((depth, WIDTH_Q), lambda i: (i, 0)),
        ] + [ANY] * len(after),
        out_specs=pl.BlockSpec((TOKENS, WIDTH_Q), lambda i: (0, 0)),
        out_shape=jax.ShapeDtypeStruct((TOKENS, WIDTH_Q), bf16),
        scratch_shapes=[pltpu.VMEM((depth, WIDTH_Q), bf16), pltpu.VMEM((TOKENS, WIDTH_Q), f32)],
        cost_estimate=pl.CostEstimate(flops=2 * 256 * 7168 * 512, bytes_accessed=11 * 2 ** 20, transcendentals=0),
        compiler_params=pltpu.CompilerParams(vmem_limit_bytes=VMEM),
    )(scales, hidden, panel, *after)


def choose(gate, their_gate, held, after):
    def body(gate_ref, their_ref, *refs):
        kv = refs[:4] + (refs[4:6],) + refs[6:9]
        own_ref, for_ref = refs[-2:]
        c = lax.axis_index("ctx")
        for s in range(NSLOT):
            for ref, out, hi in ((gate_ref, own_ref, c // 8), (their_ref, for_ref, 0)):
                block = ref[0, 1 + s]
                wanted = (ref[1, 1 + s] == 1) & (block // 8 == hi)
                at = jnp.where(wanted, (c + 8 - block % 8) % 8, 0)
                for j in range(8):
                    @pl.when(at == j)
                    def _(s=s, j=j, out=out):
                        if j == 4:
                            out[s, :128] = kv[4][0][...]
                            out[s, 128:] = kv[4][1][...]
                        else:
                            out[s] = kv[j][...]

    shape = jax.ShapeDtypeStruct((NSLOT, TOKENS, 2 * HD), bf16)
    return pl.pallas_call(
        body,
        in_specs=[SM, SM] + [VM] * 9 + [ANY] * len(after),
        out_specs=[VM, VM],
        out_shape=[shape, shape],
        compiler_params=pltpu.CompilerParams(vmem_limit_bytes=VMEM),
    )(gate, their_gate, *held, *after)


def merge(gate, own, got, after):
    def body(gate_ref, own_ref, got_ref, *rest):
        out_ref = rest[-1]
        hi = lax.axis_index("ctx") // 8
        for s in range(NSLOT):
            here = gate_ref[0, 1 + s] // 8 == hi

            @pl.when(here)
            def _(s=s):
                out_ref[s] = own_ref[s]

            @pl.when(jnp.logical_not(here))
            def _(s=s):
                out_ref[s] = got_ref[s]

    return pl.pallas_call(
        body,
        in_specs=[SM, VM, VM] + [ANY] * len(after),
        out_specs=VM,
        out_shape=jax.ShapeDtypeStruct((NSLOT, TOKENS, 2 * HD), bf16),
        compiler_params=pltpu.CompilerParams(vmem_limit_bytes=VMEM),
    )(gate, own, got, *after)


ROWS = TOKENS * HEADS


def attend(gate, queries, pieces, groups, states, halves, after=()):
    first = states is None
    n_state = 3 * len(halves)
    n_in = 0 if first else n_state

    def body(gate_ref, own_q_ref, sib_q_ref, *refs):
        kv = refs[:len(pieces)]
        out = refs[-n_state:]
        if not first:
            before = refs[len(pieces):len(pieces) + n_state]
        x_lo, y, core = spot()
        for at, half in enumerate(halves):
            peak, total, accum = out[3 * at:3 * at + 3]
            if first:
                peak[...] = jnp.full_like(peak, LOW)
                total[...] = jnp.zeros_like(total)
                accum[...] = jnp.zeros_like(accum)
            else:
                for ref, held in zip((peak, total, accum), before[3 * at:3 * at + 3]):
                    ref[...] = held[...]
            q_tile = (own_q_ref if half == 0 else sib_q_ref)[...]
            q = jnp.concatenate([q_tile[:, h * HD:(h + 1) * HD] for h in range(HEADS)], axis=0)
            holder = chip_at(x_lo, y, 0, 0) * 2 + (core if half == 0 else 1 - core)

            def switched(flag):
                if isinstance(flag, int):
                    on = gate_ref[1, 1 + flag] == 1
                else:
                    shard = chip_at(x_lo, y, *flag) * 2 + core
                    on = (shard < holder) | ((shard == holder) & (half == 0))
                return jnp.where(on, 0.0, LOW).astype(f32)

            for members in groups:
                ts = []
                for flag, piece, index in members:
                    t = lax.dot_general(q, kv[piece][index, :, :HD], (((1,), (1,)), ((), ())),
                                        preferred_element_type=f32) * LOG2_SCALE
                    if flag == (0, 0) and half == 0:
                        row = lax.broadcasted_iota(jnp.int32, t.shape, 0) % TOKENS
                        t = jnp.where(lax.broadcasted_iota(jnp.int32, t.shape, 1) <= row, t, LOW)
                    else:
                        t = t + switched(flag)
                    ts.append(t)
                top = ts[0]
                for t in ts[1:]:
                    top = jnp.maximum(top, t)
                top = jnp.max(jnp.maximum(top[:, :HD], top[:, HD:]), axis=1, keepdims=True)
                old = peak[...]
                new = jnp.maximum(old, jnp.broadcast_to(top, old.shape))
                fade = jnp.exp2(old - new)
                both = jnp.concatenate([new, new], axis=1)
                sums = added = None
                for t, (_, piece, index) in zip(ts, members):
                    w = jnp.exp2(t - both)
                    part = w[:, :HD] + w[:, HD:]
                    d = jnp.dot(w.astype(bf16), kv[piece][index, :, HD:], preferred_element_type=f32)
                    sums = part if sums is None else sums + part
                    added = d if added is None else added + d
                peak[...] = new
                total[...] = total[...] * fade + sums
                accum[...] = accum[...] * fade + added

    n_keys = sum(len(m) for m in groups) * TOKENS
    rows = ROWS * len(halves)
    flat = [] if first else [a for state in states for a in state]
    got = pl.pallas_call(
        body,
        in_specs=[SM, VM, VM] + [VM] * (len(pieces) + n_in) + [ANY] * len(after),
        out_specs=[VM] * n_state,
        out_shape=[jax.ShapeDtypeStruct((ROWS, HD), f32)] * n_state,
        input_output_aliases={} if first else {3 + len(pieces) + n: n for n in range(n_state)},
        cost_estimate=pl.CostEstimate(
            flops=4 * rows * n_keys * HD, bytes_accessed=6 * 2 ** 20, transcendentals=rows * n_keys),
        compiler_params=pltpu.CompilerParams(vmem_limit_bytes=VMEM),
    )(gate, *queries, *pieces, *flat, *after)
    return [got[3 * n:3 * n + 3] for n in range(len(halves))]


def finish(state, got):
    def body(p1, l1, a1, p2, l2, a2, out_ref):
        new = jnp.maximum(p1[...], p2[...])
        f1, f2 = jnp.exp2(p1[...] - new), jnp.exp2(p2[...] - new)
        total = jnp.sum(l1[...] * f1 + l2[...] * f2, axis=1, keepdims=True)
        out = (a1[...] * f1 + a2[...] * f2) / total
        for h in range(HEADS):
            out_ref[:, h * HD:(h + 1) * HD] = out[h * TOKENS:(h + 1) * TOKENS].astype(bf16)

    return pl.pallas_call(
        body,
        in_specs=[VM] * 6,
        out_specs=VM,
        out_shape=jax.ShapeDtypeStruct((TOKENS, WIDTH_Q), bf16),
        compiler_params=pltpu.CompilerParams(vmem_limit_bytes=VMEM),
    )(*state, *got)


def packed(parts, outs, dtype=bf16, after=()):
    shapes = []
    for pieces in outs:
        rows = sum(piece[2] for piece in pieces)
        shapes.append((rows,) + tuple(parts[pieces[0][0]].shape[1:]))

    def body(*refs):
        for out, pieces in zip(refs[len(parts) + len(after):], outs):
            at = 0
            for part, first, rows in pieces:
                out[at:at + rows] = refs[part][first:first + rows]
                at += rows

    return pl.pallas_call(
        body,
        in_specs=[VM] * len(parts) + [ANY] * len(after),
        out_specs=[VM] * len(outs),
        out_shape=[jax.ShapeDtypeStruct(shape, dtype) for shape in shapes],
        compiler_params=pltpu.CompilerParams(vmem_limit_bytes=VMEM),
    )(*parts, *after)


def split_panel(panel):
    def body(panel_ref, own_ref, top_ref, low_ref, queries_ref):
        own_ref[...] = panel_ref[:, WIDTH_Q:]
        top_ref[...] = panel_ref[:224, WIDTH_Q:]
        low_ref[...] = panel_ref[224:, WIDTH_Q:]
        queries_ref[...] = panel_ref[:, :WIDTH_Q]

    shapes = [(448, 2 * HD), (224, 2 * HD), (224, 2 * HD), (448, WIDTH_Q)]
    return pl.pallas_call(
        body,
        in_specs=[VM],
        out_specs=[VM] * 4,
        out_shape=[jax.ShapeDtypeStruct(shape, bf16) for shape in shapes],
        compiler_params=pltpu.CompilerParams(vmem_limit_bytes=VMEM),
    )(panel)


def released(held, after):
    def body(held_ref, after_ref, out_ref):
        pass

    return pl.pallas_call(
        body,
        in_specs=[ANY, ANY],
        out_specs=ANY,
        out_shape=jax.ShapeDtypeStruct(held.shape, held.dtype),
        input_output_aliases={0: 0},
        compiler_params=pltpu.CompilerParams(vmem_limit_bytes=VMEM),
    )(held, after)


PANEL_LAYOUT = [
    [(0, 448, 0, 0)], [(0, 448, 1, 0)], [(0, 448, 2, 0)], [(0, 448, 3, 0)],
    [(0, 224, 4, 0)], [(0, 224, 4, 224)],
    [(0, 224, 5, 0), (224, 224, 6, 0), (448, 224, 7, 0)],
    [(0, 224, 5, 224), (224, 224, 6, 224), (448, 224, 7, 224)],
]


def local(hidden, qkv_panel, qkv_scale, gate_blocks, gate_live):
    scales = qkv_scale.astype(f32)
    gate = jnp.concatenate([gate_blocks, gate_live], axis=0)

    own, top, low, q_columns = split_panel(qkv_panel)
    sib_hidden = by_plane(hidden, dcore=1)
    their_gate = across(gate, 1)
    below, above = by_plane(own, dy=1), by_plane(own, dy=-1)
    x_top, x_low = by_x(top, 1), by_x(low, -1)
    far = by_plane(own, dy=2)
    tops, lows = packed([below, above, far], [[(n, 0, 224) for n in range(3)], [(n, 224, 224) for n in range(3)]],
                        after=[x_top, x_low])
    g_top, g_low = by_x(tops, 1), by_x(lows, -1)
    q_panel = lax.all_gather(released(q_columns, tops), "fsdp", axis=0, tiled=True)
    sums = kv_project(scales, hidden, sib_hidden, [own, below, above, far, x_top, x_low], PANEL_LAYOUT[:6],
                      [0, 1, 2, 3, 4], [], [])
    mine, theirs = kv_project(scales, hidden, sib_hidden, [g_top, g_low], PANEL_LAYOUT[6:], [5, 6, 7], sums, [their_gate])
    kv = (mine + by_plane(theirs, dcore=1)).astype(bf16)

    z1, z7 = by_z(kv, 1), by_z(kv, -1)
    z2, z6 = by_z(kv, 2), by_z(kv, -2)
    z3, z5 = by_z(z2, 1), by_z(z6, -1)
    z4_top, z4_low = by_z(z2[:128], 2), by_z(z6[128:], -2)

    own_kv, for_partner = choose(gate, their_gate, [kv, z1, z2, z3, z4_top, z4_low, z5, z6, z7], [])

    kv1 = released(kv, for_partner)[None]
    below, above, beside, far = by_plane(kv1, dy=1), by_plane(kv1, dy=-1), by_plane(kv1, dx=1), by_plane(kv1, dy=2)
    packed_pair, = packed([below, above], [[(0, 0, 1), (1, 0, 1)]])
    pair, corner = by_plane(packed_pair, dx=1), by_plane(beside, dy=2)
    near = [kv1, below, above, beside, far, pair, corner]

    chosen = merge(gate, own_kv, across(for_partner, 0), [packed_pair, beside, far])
    below, above, beside = by_plane(chosen, dy=1), by_plane(chosen, dy=-1), by_plane(chosen, dx=1)
    q = q_project(scales, hidden, q_panel, [chosen])
    queries = (q, by_plane(q, dcore=1))
    packed_pair, beside2, chosen2 = packed(
        [below, above, beside, chosen],
        [[(0, 0, NSLOT), (1, 0, NSLOT)], [(2, 0, NSLOT)], [(3, 0, NSLOT)]], after=[queries[1], pair, corner])
    held = near + [chosen, below, above, beside]
    states = attend(gate, queries, held,
                    [[((0, 0), 0, 0), ((0, -1), 1, 0), ((0, 1), 2, 0), ((1, 0), 3, 0)],
                     [((0, 2), 4, 0), ((1, -1), 5, 0), ((1, 1), 5, 1), ((1, 2), 6, 0)]]
                    + [[(s, 7 + n, s) for n in range(4)] for s in range(NSLOT)],
                    None, (0, 1), after=[packed_pair])
    pair, corner, far = by_plane(packed_pair, dx=1), by_plane(beside2, dy=2), by_plane(chosen2, dy=2)
    rest = [far, pair, corner]
    groups = [[(s, 0, s), (s, 1, s), (s, 1, NSLOT + s), (s, 2, s)] for s in range(NSLOT)]
    sent, = attend(gate, queries, rest, groups, states[1:], (1,))
    got = [by_plane(a, dcore=1) for a in sent]
    kept, = attend(gate, queries, rest, groups, states[:1], (0,), after=sent[:1])
    return finish(kept, got)


def solution(mesh):
    placed = (P(("ctx", "fsdp"), None), P("fsdp", None), P(), P("ctx", None), P("ctx", None))
    return jax.shard_map(
        local, mesh=mesh, in_specs=placed, out_specs=P(("ctx", "fsdp"), None), check_vma=False
    )
```
